32 devices in a mesh: freq: 4 (over y, x), line: 8 (over z, core).
Axes of the slice: x: 2, y: 2, z: 4, core: 2. Of those that a mesh axis runs over, the one named last changes fastest.
Arguments:
- field: float32 [4, 2, 4, 24, 64, 256], P('freq', None, None, None, 'line'), may hold values from -6 to 6
- live_count: int32 [64], P('line'), may hold values from 64 to 256
- line_owner: int32 [64], replicated, may hold values from 0 to 63, each once
- decomposer: float32 [4, 2, 4, 4, 64, 256], P('freq', None, None, None, 'line'), may hold values from -1.4 to 2.4
- reflection: bfloat16 [4, 256, 2, 16384], P('freq', None, None, 'line'), may hold values from -0.046875 to 0.046875
- direct_wave: float32 [256, 4, 2, 96], P('line', 'freq'), may hold values from -6 to 6
Outputs:
- focusing: float32 [256, 4, 2, 96], P('line', 'freq')
- trace_energy: float32 [256], P('line')
The draws below stay inside these ranges and needn't reach their ends.
Inputs may be any that keep to these rules, and one draw needn't show every extreme that they name: `line_owner`: each crossline position appears once.
All inputs are finite; a program needn't handle non-finite values.
Results may differ from the reference program's by a relative error of at most 0.0023.
Values may be sent and summed in bfloat16 or wider, within the bound.
A program may use at most 64 MiB of HBM per device.

```python
import math
import jax
import jax.numpy as jnp
from jax import lax

LINES = 64
RCV = 256
FREQS = 4
FOCI = 24
SRC = 256


def draw_decomposer(key, part):
    shape = (FREQS, 2, 4, 4, LINES, RCV)
    noise = jnp.clip(0.35 * jax.random.normal(key, shape, jnp.float32), -1.4, 1.4)
    identity = jnp.eye(4, dtype=jnp.float32)
    diagonal_part = jnp.stack([identity, jnp.zeros((4, 4), jnp.float32)])
    return noise + diagonal_part[None, :, :, :, None, None]


def touch_ends(result, key, low, high):
    shape = result.shape
    index_at = [jax.random.randint(jax.random.fold_in(key, axis), (), 0, shape[axis]) for axis in range(len(shape))]
    result = result.at[tuple(index_at)].set(low)
    longest = shape.index(max(shape))
    index_at[longest] = (index_at[longest] + 1) % shape[longest]
    return result.at[tuple(index_at)].set(high)


def raised(values, rng, source, target, parts, factor):
    def block_of(dim):
        return (jnp.arange(values.shape[dim]) // (values.shape[dim] // parts)).reshape((-1,) + (1,) * (values.ndim - 1 - dim))

    one_side = jax.random.permutation(rng, parts)[block_of(target)]
    second = (block_of(target) + parts // 2) % parts
    return jnp.where((block_of(source) == one_side) | (block_of(source) == second), factor * values, values)


def steps_of(rng, shape, cuts, smallest, top_value):
    loudness = 1.0
    for position, parts in cuts:
        draws = jax.random.uniform(jax.random.fold_in(jax.random.fold_in(rng, 6), position), (parts,), jnp.float32, smallest / len(cuts), top_value / len(cuts))
        loudness = loudness * jnp.repeat(jnp.exp(draws), shape[position] // parts).reshape((-1,) + (1,) * (len(shape) - 1 - position))
    return loudness


def normal_values(stream_key, dims, scale, reach, split=(), held_as=jnp.bfloat16):
    loudness = steps_of(stream_key, dims, split, -0.22, 0.18) if split else 1.0
    drawn = jax.random.normal(stream_key, dims, jnp.float32) * scale * loudness
    return jnp.minimum(jnp.maximum(drawn, -reach), reach).astype(held_as)


def heavy_noise(stream_key, shape, scale, most, split, heavy, kind=jnp.bfloat16):
    result = scale * jax.random.normal(stream_key, shape, jnp.float32)
    if split:
        result = result * steps_of(stream_key, shape, split, -0.22, 0.18)
    return jnp.clip(raised(result, jax.random.fold_in(stream_key, 3), *heavy), -most, most).astype(kind)


def setup_inputs(seed: int = 0) -> dict:
    key_list = jax.random.split(jax.random.key(seed), 7)
    return {
        "field": normal_values(key_list[0], (FREQS, 2, 4, FOCI, LINES, RCV), 1.0, 6.0, ((0, 4), (4, 8)), jnp.float32),
        "live_count": touch_ends(jax.random.randint(key_list[1], (LINES,), RCV // 4, RCV + 1), jax.random.fold_in(key_list[1], 1), RCV // 4, RCV).astype(jnp.int32),
        "line_owner": jax.random.permutation(key_list[2], LINES).astype(jnp.int32),
        "decomposer": draw_decomposer(jax.random.fold_in(key_list[6], 71), 0),
        "reflection": heavy_noise(key_list[4], (FREQS, SRC, 2, LINES * RCV), (2 * LINES * RCV) ** -0.5, 0.046875, ((0, 4), (3, 8)), (3, 1, 8, 2.0)),
        "direct_wave": normal_values(key_list[5], (SRC, FREQS, 2, 4 * FOCI), 1.0, 6.0, ((0, 8), (1, 4)), jnp.float32),
    }


def phase_tables(line_owner, length):
    wavenum = jnp.arange(length, dtype=jnp.int32)
    products = wavenum[:, None] * line_owner[None, :].astype(jnp.int32) % length
    angles = products.astype(jnp.float32) * (2.0 * math.pi / length)
    return (jnp.cos(angles), jnp.sin(angles))

def decompose(operator, spectrum):
    real_rows = []
    imag_rows = []
    for target in range(4):
        real_sum = None
        imag_sum = None
        for source in range(4):
            weight_real = operator[:, 0, target, source][:, None]
            weight_imag = operator[:, 1, target, source][:, None]
            field_real = spectrum[:, 0, source]
            field_imag = spectrum[:, 1, source]
            term_real = weight_real * field_real - weight_imag * field_imag
            term_imag = weight_real * field_imag + weight_imag * field_real
            real_sum = term_real if real_sum is None else real_sum + term_real
            imag_sum = term_imag if imag_sum is None else imag_sum + term_imag
        real_rows.append(real_sum)
        imag_rows.append(imag_sum)
    return jnp.stack([jnp.stack(real_rows, 1), jnp.stack(imag_rows, 1)], 1)

def reference(field, live_count, line_owner, decomposer, reflection, direct_wave):
    cosine, sine_table = phase_tables(line_owner, LINES)
    forward_table = jnp.stack([jnp.stack([cosine, sine_table]), jnp.stack([-sine_table, cosine])])
    inverse_table = jnp.stack([jnp.stack([cosine.T, -sine_table.T]), jnp.stack([sine_table.T, cosine.T])]) / LINES
    live_mask = jnp.arange(RCV, dtype=jnp.int32)[None, :] < live_count[:, None]

    def one_freq(operands):
        block, operator, panel = operands
        live_field = jnp.where(live_mask, block, jnp.float32(0.0))
        spectrum = jnp.einsum('yxkj,xiojr->yiokr', forward_table, live_field, precision=lax.Precision.HIGHEST)
        decomposed = decompose(operator[None], spectrum[None])[0]
        wavefield = jnp.einsum('yxjk,xiokr->yiojr', inverse_table, decomposed, precision=lax.Precision.HIGHEST)
        wave_bf = wavefield.astype(jnp.bfloat16).reshape(2, 4 * FOCI, LINES * RCV)
        real_part = wave_bf[0]
        imag_part = wave_bf[1]
        stacked = jnp.stack([jnp.stack([real_part, imag_part], 0), jnp.stack([-imag_part, real_part], 0)], 0)
        right_side = jnp.transpose(stacked, (0, 3, 1, 2)).reshape(2 * LINES * RCV, 8 * FOCI)
        left_side = panel.reshape(SRC, 2 * LINES * RCV)
        product = jnp.dot(left_side, right_side, preferred_element_type=jnp.float32)
        return product.reshape(SRC, 2, 4 * FOCI)
    reflected = lax.map(one_freq, (field, decomposer, reflection))
    reflected = jnp.transpose(reflected, (1, 0, 2, 3))
    focusing = direct_wave - reflected
    weights = 2.0 * jnp.arange(1, FREQS + 1, dtype=jnp.int32).astype(jnp.float32) / (FREQS * (FREQS + 1))
    energy_sum = lax.optimization_barrier(jnp.sum(lax.optimization_barrier(jnp.sum(reflected * reflected, axis=(2, 3))) * weights[None, :], axis=1))
    trace_energy = jnp.sqrt(energy_sum / (8 * FOCI) + 1e-06)
    return (focusing, trace_energy)
```

```python
import math

import jax
import jax.numpy as jnp
import numpy as np
from jax import lax
from jax.experimental import pallas as pl
from jax.experimental.pallas import tpu as pltpu
from jax.sharding import PartitionSpec as P

MESH = pl.DeviceIdType.MESH
HIGHEST = lax.Precision.HIGHEST
FIELD_SCALE = 5400.0
OPERATOR_SCALE = 13600.0


def contract(left, right, dims):
    return lax.dot_general(left, right, (dims, ((), ())), preferred_element_type=jnp.float32)


def split(value):
    high = value.astype(jnp.bfloat16)
    return high, (value - high.astype(jnp.float32)).astype(jnp.bfloat16)


def fine_dot(left, right):
    left_high, left_low = split(left)
    right_high, right_low = split(right)
    dims = ((1,), (0,))
    return contract(left_high, right_high, dims) + (
        contract(left_high, right_low, dims) + contract(left_low, right_high, dims)
    )


def coded(value, scale):
    return jnp.round(value * scale).astype(jnp.int32).astype(jnp.int16)


def update_kernel(
    freqs, parts, foci, rows_j,
    counts, field, operator, table, inverse, panel, direct, order,
    focusing, energy,
    send1, recv1, weights, spread, send2, recv2, total, recv3, shared,
    sends1, recvs1, sends2, recvs2, sends3, recvs3, sends4, recvs4, local_sem,
):
    chips = parts // 2
    group = foci // chips
    tile = 2 * rows_j
    lanes = 4 * group * 128
    outs = 8 * group
    me = lax.axis_index("line")
    freq = lax.axis_index("freq")

    barrier = pltpu.get_barrier_semaphore()
    for step in range(1, parts):
        pl.semaphore_signal(
            barrier, inc=1, device_id=(freq, lax.rem(me + step, parts)), device_id_type=MESH
        )
    for step in range(1, freqs):
        pl.semaphore_signal(
            barrier, inc=1, device_id=(lax.rem(freq + step, freqs), me), device_id_type=MESH
        )

    row = lax.broadcasted_iota(jnp.int32, (rows_j, 256), 0)
    count = jnp.zeros((rows_j, 256), jnp.int32)
    for line in range(rows_j):
        count = jnp.where(row == line, counts[line], count)
    live = lax.broadcasted_iota(jnp.int32, (rows_j, 256), 1) < count

    def pack_operator(target, carry):
        for source in range(4):
            block = coded(operator[:, target, source], OPERATOR_SCALE).reshape(tile, 256)
            at = pl.ds(pl.multiple_of(lanes + (target * 4 + source) * 128, 128), 128)
            for part in range(parts):
                send1[part, :, at] = block[:, (part % 2) * 128:(part % 2) * 128 + 128]
        return carry

    lax.fori_loop(0, 4, pack_operator, 0)

    def pack_field(focus, carry):
        for source in range(4):
            at = pl.ds(pl.multiple_of((focus * 4 + source) * 128, 128), 128)
            for chip in range(chips):
                value = field[:, source, chip * group + focus]
                value = jnp.where(live[None], value, 0.0)
                block = coded(value, FIELD_SCALE).reshape(tile, 256)
                send1[2 * chip, :, at] = block[:, :128]
                send1[2 * chip + 1, :, at] = block[:, 128:]
        return carry

    lax.fori_loop(0, group, pack_field, 0)
    pl.semaphore_wait(barrier, parts - 1 + freqs - 1)

    def rows_of(part, size):
        return pl.ds(pl.multiple_of(part * size, size), size)

    first = []
    for step in STEPS:
        peer = lax.rem(me + step, parts)
        copy = pltpu.make_async_remote_copy(
            src_ref=send1.at[peer],
            dst_ref=recv1.at[rows_of(me, tile), :],
            send_sem=sends1.at[step],
            recv_sem=recvs1.at[step],
            device_id=(freq, peer),
            device_id_type=MESH,
        )
        copy.start()
        first.append(copy)
    own = pltpu.make_async_copy(send1.at[me], recv1.at[rows_of(me, tile), :], local_sem.at[0])
    own.start()
    own.wait()
    for copy in first:
        copy.wait()

    for block in range(16):
        at = lanes + block * 128
        weights[:, block * 128:block * 128 + 128] = recv1[:, at:at + 128].astype(jnp.float32) * (
            1.0 / OPERATOR_SCALE
        )

    count_rows = parts * rows_j * 2
    step_rows = 8 * group

    def transform(focus, carry):
        at = pl.ds(pl.multiple_of(focus * 512, 512), 512)
        values = recv1[:, at].astype(jnp.float32)
        spectrum = fine_dot(table[...], values).reshape(count_rows // tile, 2, rows_j, 512)
        real, imag = spectrum[:, 0], spectrum[:, 1]
        columns = []
        for target in range(4):
            out_real, out_imag = None, None
            for source in range(4):
                lo = (target * 4 + source) * 128
                weight = weights[:, lo:lo + 128].reshape(count_rows // tile, 2, rows_j, 128)
                wr, wi = weight[:, 0], weight[:, 1]
                fr = real[:, :, source * 128:source * 128 + 128]
                fi = imag[:, :, source * 128:source * 128 + 128]
                tr = wr * fr - wi * fi
                ti = wr * fi + wi * fr
                out_real = tr if out_real is None else out_real + tr
                out_imag = ti if out_imag is None else out_imag + ti
            columns.append(jnp.stack([out_real, out_imag], 1).reshape(count_rows, 128))
        wave = fine_dot(inverse[...], jnp.concatenate(columns, 1))
        for part in range(parts):
            for comp in range(2):
                for target in range(4):
                    lo = part * tile + comp * rows_j
                    start = part * rows_j * outs + comp * 4 * group + target * group + focus
                    spread[pl.ds(start, rows_j, stride=outs), :] = wave[
                        lo:lo + rows_j, target * 128:target * 128 + 128
                    ]
        return carry

    lax.fori_loop(0, group, transform, 0)

    second = []
    chip = me // 2
    core = lax.rem(me, 2)
    land = recv2.at[core, rows_of(chip, outs), :]

    def pack_wave(part, carry):
        for line in range(rows_j):
            start = pl.multiple_of((part * rows_j + line) * outs, outs)
            send2[part, :, line * 128:line * 128 + 128] = spread[pl.ds(start, outs), :].astype(
                jnp.bfloat16
            )
        return carry

    lax.fori_loop(0, parts, pack_wave, 0)
    for step in STEPS:
        peer = lax.rem(me + step, parts)
        copy = pltpu.make_async_remote_copy(
            src_ref=send2.at[peer],
            dst_ref=land,
            send_sem=sends2.at[step],
            recv_sem=recvs2.at[step],
            device_id=(freq, peer),
            device_id_type=MESH,
        )
        copy.start()
        second.append(copy)
    own = pltpu.make_async_copy(send2.at[me], land, local_sem.at[1])
    own.start()
    own.wait()
    for copy in second:
        copy.wait()

    nt = ((1,), (1,))
    with_real = contract(recv2[0], panel[0, 0], nt) + contract(recv2[1], panel[0, 1], nt)
    with_imag = contract(recv2[0], panel[1, 0], nt) + contract(recv2[1], panel[1, 1], nt)
    half = outs // 2
    pieces = []
    for part in range(chips):
        lo = part * outs
        pieces.append(with_real[lo:lo + half] - with_imag[lo + half:lo + outs])
        pieces.append(with_real[lo + half:lo + outs] + with_imag[lo:lo + half])
    width = order.shape[0]
    if width > chips * outs:
        pieces.append(jnp.zeros((width - chips * outs, with_real.shape[1]), jnp.float32))
    total[...] = jnp.concatenate(pieces, 0).T

    sources = recv3.shape[1]
    third = []
    for step in STEPS:
        peer = lax.rem(me + step, parts)
        copy = pltpu.make_async_remote_copy(
            src_ref=total.at[rows_of(peer, sources), :],
            dst_ref=recv3.at[step],
            send_sem=sends3.at[step],
            recv_sem=recvs3.at[step],
            device_id=(freq, peer),
            device_id_type=MESH,
        )
        copy.start()
        third.append(copy)
    reflected = total[rows_of(me, sources), :]
    for copy in third:
        copy.wait()
    for step in range(1, parts):
        reflected = reflected + recv3[step]

    weight = (freq + 1).astype(jnp.float32) * (2.0 / (freqs * (freqs + 1)))
    squares = lax.dot_general(
        jnp.ones((8, width), jnp.float32),
        reflected * reflected * weight,
        (nt, ((), ())),
        precision=HIGHEST,
        preferred_element_type=jnp.float32,
    )
    if sources < 128:
        squares = jnp.concatenate([squares, jnp.zeros((8, 128 - sources), jnp.float32)], 1)
    shared[0] = squares
    fourth = []
    for step in range(1, freqs):
        copy = pltpu.make_async_remote_copy(
            src_ref=shared.at[0],
            dst_ref=shared.at[step],
            send_sem=sends4.at[step],
            recv_sem=recvs4.at[step],
            device_id=(lax.rem(freq + step, freqs), me),
            device_id_type=MESH,
        )
        copy.start()
        fourth.append(copy)
    placed = lax.dot_general(
        reflected, order[...], (((1,), (0,)), ((), ())),
        precision=HIGHEST, preferred_element_type=jnp.float32,
    )
    channels = 4 * foci
    for comp in range(2):
        lo = comp * (placed.shape[1] // 2)
        focusing[:, comp, :] = direct[:, comp, :] - placed[:, lo:lo + channels]
    for copy in fourth:
        copy.wait()
    summed = shared[0]
    for step in range(1, freqs):
        summed = summed + shared[step]
    energy[...] = jnp.sqrt(summed[:, :sources] / (2 * channels) + 1e-06)


STEPS = (4, 5, 3, 6, 2, 7, 1)


def column_order(chips, group, width):
    foci = chips * group
    result = np.zeros((width, 2 * -(-4 * foci // 128) * 128), np.float32)
    for chip in range(chips):
        for comp in range(2):
            for target in range(4):
                for focus in range(group):
                    here = ((chip * 2 + comp) * 4 + target) * group + focus
                    there = comp * (result.shape[1] // 2) + target * foci + chip * group + focus
                    result[here, there] = 1.0
    return result


def fused(field, live_count, line_owner, decomposer, reflection, direct_wave):
    freqs = lax.axis_size("freq")
    parts = lax.axis_size("line")
    foci = field.shape[3]
    rows_j = field.shape[4]
    length = line_owner.shape[0]
    chips = parts // 2
    group = foci // chips
    sources = direct_wave.shape[0]
    all_sources = reflection.shape[1]
    tile = 2 * rows_j
    lanes = 4 * group * 128
    outs = 8 * group
    width = -(-chips * outs // 128) * 128

    wavenum = jnp.arange(length, dtype=jnp.int32)
    products = wavenum[:, None] * line_owner[None, :] % length
    angles = products.astype(jnp.float32) * (2.0 * math.pi / length)
    cosine, sine = jnp.cos(angles), jnp.sin(angles)
    table = jnp.stack([jnp.stack([cosine, sine]), jnp.stack([-sine, cosine])])
    table = table.reshape(2, 2, parts, rows_j, parts, rows_j)
    table = table.transpose(2, 0, 3, 4, 1, 5).reshape(2 * length, 2 * length)
    inverse = table.T / length
    panel = reflection[0].reshape(all_sources, 2, rows_j, 2, 128).transpose(1, 3, 0, 2, 4)
    panel = panel.reshape(2, 2, all_sources, rows_j * 128)
    order = jnp.asarray(column_order(chips, group, width))

    vmem = pl.BlockSpec(memory_space=pltpu.VMEM)
    focusing, energy = pl.pallas_call(
        lambda *refs: update_kernel(freqs, parts, foci, rows_j, *refs),
        out_shape=(
            jax.ShapeDtypeStruct(direct_wave.shape[:1] + direct_wave.shape[2:], jnp.float32),
            jax.ShapeDtypeStruct((8, sources), jnp.float32),
        ),
        in_specs=[pl.BlockSpec(memory_space=pltpu.SMEM)] + [vmem] * 7,
        out_specs=(vmem, vmem),
        scratch_shapes=[
            pltpu.VMEM((parts, tile, lanes + 2048), jnp.int16),
            pltpu.VMEM((parts * tile, lanes + 2048), jnp.int16),
            pltpu.VMEM((parts * tile, 2048), jnp.float32),
            pltpu.VMEM((parts * rows_j * outs, 128), jnp.float32),
            pltpu.VMEM((parts, outs, rows_j * 128), jnp.bfloat16),
            pltpu.VMEM((2, chips * outs, rows_j * 128), jnp.bfloat16),
            pltpu.VMEM((all_sources, width), jnp.float32),
            pltpu.VMEM((parts, sources, width), jnp.float32),
            pltpu.VMEM((freqs, 8, 128), jnp.float32),
        ] + [pltpu.SemaphoreType.DMA((parts,))] * 6 + [pltpu.SemaphoreType.DMA((freqs,))] * 2
        + [pltpu.SemaphoreType.DMA((2,))],
        compiler_params=pltpu.CompilerParams(
            collective_id=0, has_side_effects=True, vmem_limit_bytes=48 * 1024 * 1024
        ),
    )(
        live_count, field[0], decomposer[0], table * (1.0 / FIELD_SCALE), inverse, panel,
        direct_wave[:, 0], order,
    )
    return focusing[:, None], energy[0]


def fits(field, line_owner, reflection, direct_wave):
    parts = lax.axis_size("line")
    rows_j = field.shape[4]
    foci = field.shape[3]
    return (
        parts == 8
        and rows_j == 8
        and field.shape[0] == 1
        and field.shape[5] == 256
        and foci % (parts // 2) == 0
        and (8 * foci // (parts // 2)) % 16 == 0
        and line_owner.shape[0] == parts * rows_j
        and direct_wave.shape[0] <= 128
        and direct_wave.shape[0] % 8 == 0
        and reflection.shape[1] <= 512
    )


def phase_tables(line_owner, length):
    wavenum = jnp.arange(length, dtype=jnp.int32)
    products = wavenum[:, None] * line_owner[None, :] % length
    angles = products.astype(jnp.float32) * (2.0 * math.pi / length)
    return (jnp.cos(angles), jnp.sin(angles))


def decompose(operator, spectrum):
    real_rows = []
    imag_rows = []
    for target in range(4):
        real_sum = None
        imag_sum = None
        for source in range(4):
            weight_real = operator[:, 0, target, source][:, None]
            weight_imag = operator[:, 1, target, source][:, None]
            field_real = spectrum[:, 0, source]
            field_imag = spectrum[:, 1, source]
            term_real = weight_real * field_real - weight_imag * field_imag
            term_imag = weight_real * field_imag + weight_imag * field_real
            real_sum = term_real if real_sum is None else real_sum + term_real
            imag_sum = term_imag if imag_sum is None else imag_sum + term_imag
        real_rows.append(real_sum)
        imag_rows.append(imag_sum)
    return jnp.stack([jnp.stack(real_rows, 1), jnp.stack(imag_rows, 1)], 1)


def general(field, live_count, line_owner, decomposer, reflection, direct_wave):
    length = line_owner.shape[0]
    receivers = field.shape[5]
    cosine, sine_table = phase_tables(line_owner, length)
    forward_table = jnp.stack([jnp.stack([cosine, sine_table]), jnp.stack([-sine_table, cosine])])
    inverse_table = (
        jnp.stack([jnp.stack([cosine.T, -sine_table.T]), jnp.stack([sine_table.T, cosine.T])])
        / length
    )
    live_mask = jnp.arange(receivers, dtype=jnp.int32)[None, :] < live_count[:, None]
    live_field = jnp.where(live_mask, field, jnp.float32(0.0))
    operator = lax.all_gather(decomposer, "line", axis=4, tiled=True)
    every_line = lax.all_to_all(live_field, "line", split_axis=3, concat_axis=4, tiled=True)
    space_all = jnp.einsum(
        "yxjk,fxiokr->fyiojr",
        inverse_table,
        decompose(
            operator,
            jnp.einsum(
                "yxkj,fxiojr->fyiokr", forward_table, every_line, precision=lax.Precision.HIGHEST
            ),
        ),
        precision=lax.Precision.HIGHEST,
    )
    wavefield = lax.all_to_all(
        space_all.astype(jnp.bfloat16), "line", split_axis=4, concat_axis=3, tiled=True
    )
    freq_count = wavefield.shape[0]
    channels = wavefield.shape[2] * wavefield.shape[3]
    positions = wavefield.shape[4] * wavefield.shape[5]
    wave_bf = wavefield.reshape(freq_count, 2, channels, positions)
    real_part = wave_bf[:, 0]
    imag_part = wave_bf[:, 1]
    stacked = jnp.stack(
        [jnp.stack([real_part, imag_part], 1), jnp.stack([-imag_part, real_part], 1)], 1
    )
    reflected = lax.psum_scatter(
        jnp.einsum("fsxq,fxocq->sfoc", reflection, stacked, preferred_element_type=jnp.float32),
        "line",
        scatter_dimension=0,
        tiled=True,
    )
    focusing = direct_wave - reflected
    total_freqs = freq_count * lax.axis_size("freq")
    freq_index = lax.axis_index("freq") * freq_count + jnp.arange(freq_count, dtype=jnp.int32)
    weights = 2.0 * (freq_index + 1).astype(jnp.float32) / (total_freqs * (total_freqs + 1))
    partial_value = jnp.sum(jnp.sum(reflected * reflected, axis=(2, 3)) * weights[None, :], axis=1)
    energy_sum = lax.psum(partial_value, "freq")
    trace_energy = jnp.sqrt(energy_sum / (2 * channels) + 1e-06)
    return (focusing, trace_energy)


def on_device(field, live_count, line_owner, decomposer, reflection, direct_wave):
    if fits(field, line_owner, reflection, direct_wave):
        body = fused
    else:
        body = general
    return body(field, live_count, line_owner, decomposer, reflection, direct_wave)


def solution(mesh):
    return jax.shard_map(
        on_device,
        mesh=mesh,
        in_specs=(
            P("freq", None, None, None, "line", None),
            P("line"),
            P(),
            P("freq", None, None, None, "line", None),
            P("freq", None, None, "line"),
            P("line", "freq", None, None),
        ),
        out_specs=(P("line", "freq", None, None), P("line")),
        check_vma=False,
    )
```

```python
import math

import jax
import jax.numpy as jnp
import numpy as np
from jax import lax
from jax.experimental import pallas as pl
from jax.experimental.pallas import tpu as pltpu
from jax.sharding import PartitionSpec as P

MESH = pl.DeviceIdType.MESH
HIGHEST = lax.Precision.HIGHEST
FIELD_SCALE = 5400.0
OPERATOR_SCALE = 13600.0


def contract(left, right, dims):
    return lax.dot_general(left, right, (dims, ((), ())), preferred_element_type=jnp.float32)


def split(value):
    high = value.astype(jnp.bfloat16)
    return high, (value - high.astype(jnp.float32)).astype(jnp.bfloat16)


def fine_dot(left, right):
    left_high, left_low = split(left)
    right_high, right_low = split(right)
    dims = ((1,), (0,))
    return contract(left_high, right_high, dims) + (
        contract(left_high, right_low, dims) + contract(left_low, right_high, dims)
    )


def coded(value, scale):
    return jnp.round(value * scale).astype(jnp.int32).astype(jnp.int16)


def update_kernel(
    freqs, parts, foci, rows_j,
    counts, owner, field_hbm, operator, panel_hbm, direct, order,
    focusing, energy,
    field, send_op, recv_op, weights, send1, recv1, tables, raw, panel, spread, send2, recv2,
    total, recv3, shared,
    sends0, recvs0, sends1, recvs1, sends2, recvs2, sends3, recvs3, sends4, recvs4, local_sem,
):
    chips = parts // 2
    group = foci // chips
    chunks = group // 2
    tile = 2 * rows_j
    length = parts * rows_j
    me = lax.axis_index("line")
    freq = lax.axis_index("freq")
    chip, core = me // 2, lax.rem(me, 2)
    peers = []
    for other in (lax.rem(chip + 2, 4), 3 - chip, chip + 1 - 2 * lax.rem(chip, 2)):
        peers.append((other, core))
        peers.append((other, 1 - core))
    peers.append((chip, 1 - core))

    loads = []
    for chunk in range(chunks):
        loads.append(
            pltpu.make_async_copy(field_hbm.at[:, :, :, chunk], field.at[chunk], local_sem.at[chunk])
        )
        loads[-1].start()
    panel_load = pltpu.make_async_copy(panel_hbm, raw, local_sem.at[chunks])
    panel_load.start()

    barrier = pltpu.get_barrier_semaphore()
    for other, side in peers:
        pl.semaphore_signal(
            barrier, inc=1, device_id=(freq, other * 2 + side), device_id_type=MESH
        )
    for step in range(1, freqs):
        pl.semaphore_signal(
            barrier, inc=1, device_id=(lax.rem(freq + step, freqs), me), device_id_type=MESH
        )

    row = lax.broadcasted_iota(jnp.int32, (rows_j, 256), 0)
    count = jnp.zeros((rows_j, 256), jnp.int32)
    for line in range(rows_j):
        count = jnp.where(row == line, counts[line], count)
    live = lax.broadcasted_iota(jnp.int32, (rows_j, 256), 1) < count

    def rows_of(part, size):
        return pl.ds(pl.multiple_of(part * size, size), size)

    mine = rows_of(me, tile)

    def send(source, target, number, sends, recvs):
        other, side = peers[number]
        copy = pltpu.make_async_remote_copy(
            src_ref=source,
            dst_ref=target,
            send_sem=sends.at[number],
            recv_sem=recvs.at[number],
            device_id=(freq, other * 2 + side),
            device_id_type=MESH,
        )
        copy.start()
        return copy

    def pack_operator(target, carry):
        for source in range(4):
            block = coded(operator[:, target, source], OPERATOR_SCALE).reshape(tile, 256)
            at = pl.ds(pl.multiple_of((target * 4 + source) * 128, 128), 128)
            send_op[0, :, at] = block[:, :128]
            send_op[1, :, at] = block[:, 128:]
        return carry

    lax.fori_loop(0, 4, pack_operator, 0)
    pl.semaphore_wait(barrier, parts - 1 + freqs - 1)
    zeroth = [
        send(send_op.at[side], recv_op.at[mine, :], number, sends0, recvs0)
        for number, (other, side) in enumerate(peers)
    ]
    recv_op[mine, :] = send_op[core]

    first = []
    for chunk in range(chunks):
        loads[chunk].wait()

        def pack_field(to, carry):
            for focus in range(2):
                for source in range(4):
                    value = jnp.where(live[None], field[chunk, :, source, to, focus], 0.0)
                    block = coded(value, FIELD_SCALE).reshape(tile, 256)
                    lo = (focus * 4 + source) * 128
                    send1[chunk, 2 * to, :, lo:lo + 128] = block[:, :128]
                    send1[chunk, 2 * to + 1, :, lo:lo + 128] = block[:, 128:]
            return carry

        lax.fori_loop(0, chips, pack_field, 0)
        first.append([
            send(send1.at[chunk, other * 2 + side], recv1.at[chunk, mine, :], number,
                 sends1.at[chunk], recvs1.at[chunk])
            for number, (other, side) in enumerate(peers)
        ])
        recv1[chunk, mine, :] = send1[chunk, me]

    column = lax.broadcasted_iota(jnp.int32, (length, 2 * length), 1)
    line = column // tile * rows_j + lax.rem(column, rows_j)
    pick = line == lax.broadcasted_iota(jnp.int32, (length, 2 * length), 0)
    owners = contract(
        jnp.broadcast_to(owner[...].astype(jnp.float32).astype(jnp.bfloat16), (8, length)),
        pick.astype(jnp.float32).astype(jnp.bfloat16),
        ((1,), (0,)),
    )[:1].astype(jnp.int32)
    across = lax.broadcasted_iota(jnp.int32, (2 * length, 2 * length), 1)
    down = lax.broadcasted_iota(jnp.int32, (2 * length, 2 * length), 0)
    wavenum = down // tile * rows_j + lax.rem(down, rows_j)
    quarter = lax.rem(down, tile) // rows_j - lax.rem(across, tile) // rows_j
    turns = lax.rem(wavenum * owners + (quarter + 4) * (length // 4), length)
    wheel = jnp.cos(turns.astype(jnp.float32) * (2.0 * math.pi / length))
    tables[0] = wheel * (1.0 / FIELD_SCALE)
    tables[1] = wheel.T * (1.0 / length)

    panel_load.wait()
    all_sources = raw.shape[0]

    def unpack_panel(block, carry):
        at = pl.ds(pl.multiple_of(block * 16, 16), 16)
        values = raw[at].astype(jnp.float32)
        for comp in range(2):
            half = values[:, comp, :].astype(jnp.bfloat16)
            for line in range(rows_j):
                for side in range(2):
                    lo = (line * 2 + side) * 128
                    panel[comp, side, at, line * 128:line * 128 + 128] = half[:, lo:lo + 128]
        return carry

    lax.fori_loop(0, all_sources // 16, unpack_panel, 0)

    for copy in zeroth:
        copy.wait()
    for block in range(16):
        lo = block * 128
        weights[:, lo:lo + 128] = recv_op[:, lo:lo + 128].astype(jnp.float32) * (
            1.0 / OPERATOR_SCALE
        )

    second = []
    land_rows = rows_of(chip, 16)
    for chunk in range(chunks):
        for copy in first[chunk]:
            copy.wait()

        def transform(focus, carry):
            at = pl.ds(pl.multiple_of(focus * 512, 512), 512)
            values = recv1[chunk, :, at].astype(jnp.float32)
            spectrum = fine_dot(tables[0], values).reshape(parts, 2, rows_j, 512)
            real, imag = spectrum[:, 0], spectrum[:, 1]
            columns = []
            for target in range(4):
                out_real, out_imag = None, None
                for source in range(4):
                    lo = (target * 4 + source) * 128
                    weight = weights[:, lo:lo + 128].reshape(parts, 2, rows_j, 128)
                    wr, wi = weight[:, 0], weight[:, 1]
                    fr = real[:, :, source * 128:source * 128 + 128]
                    fi = imag[:, :, source * 128:source * 128 + 128]
                    tr = wr * fr - wi * fi
                    ti = wr * fi + wi * fr
                    out_real = tr if out_real is None else out_real + tr
                    out_imag = ti if out_imag is None else out_imag + ti
                columns.append(jnp.stack([out_real, out_imag], 1).reshape(2 * length, 128))
            wave = fine_dot(tables[1], jnp.concatenate(columns, 1))
            for part in range(parts):
                for comp in range(2):
                    for target in range(4):
                        lo = part * tile + comp * rows_j
                        start = part * rows_j * 16 + comp * 8 + target * 2 + focus
                        spread[pl.ds(start, rows_j, stride=16), :] = wave[
                            lo:lo + rows_j, target * 128:target * 128 + 128
                        ]
            return carry

        lax.fori_loop(0, 2, transform, 0)

        def pack_wave(part, carry):
            for line in range(rows_j):
                start = pl.multiple_of((part * rows_j + line) * 16, 16)
                send2[chunk, part, :, line * 128:line * 128 + 128] = spread[
                    pl.ds(start, 16), :
                ].astype(jnp.bfloat16)
            return carry

        lax.fori_loop(0, parts, pack_wave, 0)
        second.append([
            send(send2.at[chunk, other * 2 + side], recv2.at[chunk, core, land_rows, :], number,
                 sends2.at[chunk], recvs2.at[chunk])
            for number, (other, side) in enumerate(peers)
        ])
        recv2[chunk, core, land_rows, :] = send2[chunk, me]

    nt = ((1,), (1,))
    pieces = []
    for chunk in range(chunks):
        for copy in second[chunk]:
            copy.wait()
        wave0, wave1 = recv2[chunk, 0], recv2[chunk, 1]
        with_real = contract(wave0, panel[0, 0], nt) + contract(wave1, panel[0, 1], nt)
        with_imag = contract(wave0, panel[1, 0], nt) + contract(wave1, panel[1, 1], nt)
        for part in range(chips):
            lo = part * 16
            pieces.append(with_real[lo:lo + 8] - with_imag[lo + 8:lo + 16])
            pieces.append(with_real[lo + 8:lo + 16] + with_imag[lo:lo + 8])
    width = order.shape[0]
    if width > 8 * foci:
        pieces.append(jnp.zeros((width - 8 * foci, all_sources), jnp.float32))
    total[...] = jnp.concatenate(pieces, 0).T

    sources = recv3.shape[1]
    third = [
        send(total.at[rows_of(other * 2 + side, sources), :], recv3.at[number], number,
             sends3, recvs3)
        for number, (other, side) in enumerate(peers)
    ]
    reflected = total[rows_of(me, sources), :]
    for number, copy in enumerate(third):
        copy.wait()
    for number in range(parts - 1):
        reflected = reflected + recv3[number]

    weight = (freq + 1).astype(jnp.float32) * (2.0 / (freqs * (freqs + 1)))
    squares = lax.dot_general(
        jnp.ones((8, width), jnp.float32),
        reflected * reflected * weight,
        (nt, ((), ())),
        precision=HIGHEST,
        preferred_element_type=jnp.float32,
    )
    if sources < 128:
        squares = jnp.concatenate([squares, jnp.zeros((8, 128 - sources), jnp.float32)], 1)
    shared[0] = squares
    fourth = []
    for step in range(1, freqs):
        copy = pltpu.make_async_remote_copy(
            src_ref=shared.at[0],
            dst_ref=shared.at[step],
            send_sem=sends4.at[step],
            recv_sem=recvs4.at[step],
            device_id=(lax.rem(freq + step, freqs), me),
            device_id_type=MESH,
        )
        copy.start()
        fourth.append(copy)
    placed = lax.dot_general(
        reflected, order[...], (((1,), (0,)), ((), ())),
        precision=HIGHEST, preferred_element_type=jnp.float32,
    )
    channels = 4 * foci
    for comp in range(2):
        lo = comp * (placed.shape[1] // 2)
        focusing[:, comp, :] = direct[:, comp, :] - placed[:, lo:lo + channels]
    for copy in fourth:
        copy.wait()
    summed = shared[0]
    for step in range(1, freqs):
        summed = summed + shared[step]
    energy[...] = jnp.sqrt(summed[:1, :sources] / (2 * channels) + 1e-06)


def column_order(chips, group, width):
    foci = chips * group
    result = np.zeros((width, 2 * -(-4 * foci // 128) * 128), np.float32)
    here = 0
    for chunk in range(group // 2):
        for chip in range(chips):
            for comp in range(2):
                for target in range(4):
                    for focus in range(2):
                        at = target * foci + chip * group + chunk * 2 + focus
                        result[here, comp * (result.shape[1] // 2) + at] = 1.0
                        here += 1
    return result


def fused(field, live_count, line_owner, decomposer, reflection, direct_wave):
    freqs = lax.axis_size("freq")
    parts = lax.axis_size("line")
    foci = field.shape[3]
    rows_j = field.shape[4]
    length = line_owner.shape[0]
    chips = parts // 2
    group = foci // chips
    chunks = group // 2
    sources = direct_wave.shape[0]
    all_sources = reflection.shape[1]
    tile = 2 * rows_j
    width = -(-8 * foci // 128) * 128
    order = jnp.asarray(column_order(chips, group, width))

    vmem = pl.BlockSpec(memory_space=pltpu.VMEM)
    smem = pl.BlockSpec(memory_space=pltpu.SMEM)
    far = pl.BlockSpec(memory_space=pl.ANY)
    pair = pltpu.SemaphoreType.DMA((parts - 1,))
    many = pltpu.SemaphoreType.DMA((chunks, parts - 1))
    focusing, energy = pl.pallas_call(
        lambda *refs: update_kernel(freqs, parts, foci, rows_j, *refs),
        out_shape=(
            jax.ShapeDtypeStruct(direct_wave.shape[:1] + direct_wave.shape[2:], jnp.float32),
            jax.ShapeDtypeStruct((1, sources), jnp.float32),
        ),
        in_specs=[smem, vmem, far, vmem, far, vmem, vmem],
        out_specs=(vmem, vmem),
        scratch_shapes=[
            pltpu.VMEM((chunks, 2, 4, chips, 2, rows_j, 256), jnp.float32),
            pltpu.VMEM((2, tile, 2048), jnp.int16),
            pltpu.VMEM((parts * tile, 2048), jnp.int16),
            pltpu.VMEM((parts * tile, 2048), jnp.float32),
            pltpu.VMEM((chunks, parts, tile, 1024), jnp.int16),
            pltpu.VMEM((chunks, parts * tile, 1024), jnp.int16),
            pltpu.VMEM((2, 2 * length, 2 * length), jnp.float32),
            pltpu.VMEM(reflection.shape[1:], jnp.bfloat16),
            pltpu.VMEM((2, 2, all_sources, rows_j * 128), jnp.bfloat16),
            pltpu.VMEM((parts * rows_j * 16, 128), jnp.float32),
            pltpu.VMEM((chunks, parts, 16, rows_j * 128), jnp.bfloat16),
            pltpu.VMEM((chunks, 2, chips * 16, rows_j * 128), jnp.bfloat16),
            pltpu.VMEM((all_sources, width), jnp.float32),
            pltpu.VMEM((parts - 1, sources, width), jnp.float32),
            pltpu.VMEM((freqs, 8, 128), jnp.float32),
            pair, pair, many, many, many, many, pair, pair,
            pltpu.SemaphoreType.DMA((freqs,)),
            pltpu.SemaphoreType.DMA((freqs,)),
            pltpu.SemaphoreType.DMA((chunks + 1,)),
        ],
        compiler_params=pltpu.CompilerParams(
            collective_id=0, has_side_effects=True, vmem_limit_bytes=48 * 1024 * 1024
        ),
    )(
        live_count,
        line_owner[None],
        field.reshape(2, 4, chips, chunks, 2, rows_j, 256),
        decomposer[0],
        reflection[0],
        direct_wave[:, 0],
        order,
    )
    return focusing[:, None], energy[0]


def fits(field, line_owner, reflection, direct_wave):
    parts = lax.axis_size("line")
    rows_j = field.shape[4]
    foci = field.shape[3]
    return (
        parts == 8
        and rows_j == 8
        and field.shape[0] == 1
        and field.shape[5] == 256
        and foci % parts == 0
        and line_owner.shape[0] == parts * rows_j
        and direct_wave.shape[0] <= 128
        and direct_wave.shape[0] % 8 == 0
        and reflection.shape[1] % 256 == 0
        and reflection.shape[1] <= 512
    )


def phase_tables(line_owner, length):
    wavenum = jnp.arange(length, dtype=jnp.int32)
    products = wavenum[:, None] * line_owner[None, :] % length
    angles = products.astype(jnp.float32) * (2.0 * math.pi / length)
    return (jnp.cos(angles), jnp.sin(angles))


def decompose(operator, spectrum):
    real_rows = []
    imag_rows = []
    for target in range(4):
        real_sum = None
        imag_sum = None
        for source in range(4):
            weight_real = operator[:, 0, target, source][:, None]
            weight_imag = operator[:, 1, target, source][:, None]
            field_real = spectrum[:, 0, source]
            field_imag = spectrum[:, 1, source]
            term_real = weight_real * field_real - weight_imag * field_imag
            term_imag = weight_real * field_imag + weight_imag * field_real
            real_sum = term_real if real_sum is None else real_sum + term_real
            imag_sum = term_imag if imag_sum is None else imag_sum + term_imag
        real_rows.append(real_sum)
        imag_rows.append(imag_sum)
    return jnp.stack([jnp.stack(real_rows, 1), jnp.stack(imag_rows, 1)], 1)


def general(field, live_count, line_owner, decomposer, reflection, direct_wave):
    length = line_owner.shape[0]
    receivers = field.shape[5]
    cosine, sine_table = phase_tables(line_owner, length)
    forward_table = jnp.stack([jnp.stack([cosine, sine_table]), jnp.stack([-sine_table, cosine])])
    inverse_table = (
        jnp.stack([jnp.stack([cosine.T, -sine_table.T]), jnp.stack([sine_table.T, cosine.T])])
        / length
    )
    live_mask = jnp.arange(receivers, dtype=jnp.int32)[None, :] < live_count[:, None]
    live_field = jnp.where(live_mask, field, jnp.float32(0.0))
    operator = lax.all_gather(decomposer, "line", axis=4, tiled=True)
    every_line = lax.all_to_all(live_field, "line", split_axis=3, concat_axis=4, tiled=True)
    space_all = jnp.einsum(
        "yxjk,fxiokr->fyiojr",
        inverse_table,
        decompose(
            operator,
            jnp.einsum(
                "yxkj,fxiojr->fyiokr", forward_table, every_line, precision=lax.Precision.HIGHEST
            ),
        ),
        precision=lax.Precision.HIGHEST,
    )
    wavefield = lax.all_to_all(
        space_all.astype(jnp.bfloat16), "line", split_axis=4, concat_axis=3, tiled=True
    )
    freq_count = wavefield.shape[0]
    channels = wavefield.shape[2] * wavefield.shape[3]
    positions = wavefield.shape[4] * wavefield.shape[5]
    wave_bf = wavefield.reshape(freq_count, 2, channels, positions)
    real_part = wave_bf[:, 0]
    imag_part = wave_bf[:, 1]
    stacked = jnp.stack(
        [jnp.stack([real_part, imag_part], 1), jnp.stack([-imag_part, real_part], 1)], 1
    )
    reflected = lax.psum_scatter(
        jnp.einsum("fsxq,fxocq->sfoc", reflection, stacked, preferred_element_type=jnp.float32),
        "line",
        scatter_dimension=0,
        tiled=True,
    )
    focusing = direct_wave - reflected
    total_freqs = freq_count * lax.axis_size("freq")
    freq_index = lax.axis_index("freq") * freq_count + jnp.arange(freq_count, dtype=jnp.int32)
    weights = 2.0 * (freq_index + 1).astype(jnp.float32) / (total_freqs * (total_freqs + 1))
    partial_value = jnp.sum(jnp.sum(reflected * reflected, axis=(2, 3)) * weights[None, :], axis=1)
    energy_sum = lax.psum(partial_value, "freq")
    trace_energy = jnp.sqrt(energy_sum / (2 * channels) + 1e-06)
    return (focusing, trace_energy)


def on_device(field, live_count, line_owner, decomposer, reflection, direct_wave):
    if fits(field, line_owner, reflection, direct_wave):
        body = fused
    else:
        body = general
    return body(field, live_count, line_owner, decomposer, reflection, direct_wave)


def solution(mesh):
    return jax.shard_map(
        on_device,
        mesh=mesh,
        in_specs=(
            P("freq", None, None, None, "line", None),
            P("line"),
            P(),
            P("freq", None, None, None, "line", None),
            P("freq", None, None, "line"),
            P("line", "freq", None, None),
        ),
        out_specs=(P("line", "freq", None, None), P("line")),
        check_vma=False,
    )
```

```python
import math

import jax
import jax.numpy as jnp
import numpy as np
from jax import lax
from jax.experimental import pallas as pl
from jax.experimental.pallas import tpu as pltpu
from jax.sharding import PartitionSpec as P

MESH = pl.DeviceIdType.MESH
HIGHEST = lax.Precision.HIGHEST
FIELD_SCALE = 5400.0
OPERATOR_SCALE = 13600.0


def contract(left, right, dims):
    return lax.dot_general(left, right, (dims, ((), ())), preferred_element_type=jnp.float32)


def split(value):
    high = value.astype(jnp.bfloat16)
    return high, (value - high.astype(jnp.float32)).astype(jnp.bfloat16)


def fine_dot(left, right):
    left_high, left_low = split(left)
    right_high, right_low = split(right)
    dims = ((1,), (0,))
    return contract(left_high, right_high, dims) + (
        contract(left_high, right_low, dims) + contract(left_low, right_high, dims)
    )


def coded(value, scale):
    return jnp.round(value * scale).astype(jnp.int32).astype(jnp.int16)


def update_kernel(
    freqs, parts, foci, rows_j,
    counts, owner, field_hbm, operator, panel_hbm, direct, order,
    focusing, energy,
    field, send_op, recv_op, weights, send1, recv1, tables, raw, panel, spread, send2, recv2,
    total, twin, joined, recv3, shared,
    sends0, recvs0, sends1, recvs1, sends2, recvs2, sends3, recvs3, sends4, recvs4, local_sem,
):
    chips = parts // 2
    group = foci // chips
    chunks = group // 2
    tile = 2 * rows_j
    length = parts * rows_j
    me = lax.axis_index("line")
    freq = lax.axis_index("freq")
    chip, core = me // 2, lax.rem(me, 2)
    peers = []
    for other in (lax.rem(chip + 2, 4), 3 - chip, chip + 1 - 2 * lax.rem(chip, 2)):
        peers.append((other, core))
        peers.append((other, 1 - core))
    peers.append((chip, 1 - core))

    loads = []
    for chunk in range(chunks):
        loads.append(
            pltpu.make_async_copy(field_hbm.at[:, :, :, chunk], field.at[chunk], local_sem.at[chunk])
        )
        loads[-1].start()
    panel_load = pltpu.make_async_copy(panel_hbm, raw, local_sem.at[chunks])
    panel_load.start()

    barrier = pltpu.get_barrier_semaphore()
    for other, side in peers:
        pl.semaphore_signal(
            barrier, inc=1, device_id=(freq, other * 2 + side), device_id_type=MESH
        )
    for step in range(1, freqs):
        pl.semaphore_signal(
            barrier, inc=1, device_id=(lax.rem(freq + step, freqs), me), device_id_type=MESH
        )

    row = lax.broadcasted_iota(jnp.int32, (rows_j, 256), 0)
    count = jnp.zeros((rows_j, 256), jnp.int32)
    for line in range(rows_j):
        count = jnp.where(row == line, counts[line], count)
    live = lax.broadcasted_iota(jnp.int32, (rows_j, 256), 1) < count

    def rows_of(part, size):
        return pl.ds(pl.multiple_of(part * size, size), size)

    mine = rows_of(me, tile)

    def send(source, target, number, sends, recvs):
        other, side = peers[number]
        copy = pltpu.make_async_remote_copy(
            src_ref=source,
            dst_ref=target,
            send_sem=sends.at[number],
            recv_sem=recvs.at[number],
            device_id=(freq, other * 2 + side),
            device_id_type=MESH,
        )
        copy.start()
        return copy

    def pack_operator(target, carry):
        for source in range(4):
            block = coded(operator[:, target, source], OPERATOR_SCALE).reshape(tile, 256)
            at = pl.ds(pl.multiple_of((target * 4 + source) * 128, 128), 128)
            send_op[0, :, at] = block[:, :128]
            send_op[1, :, at] = block[:, 128:]
        return carry

    lax.fori_loop(0, 4, pack_operator, 0)
    pl.semaphore_wait(barrier, parts - 1 + freqs - 1)
    zeroth = [
        send(send_op.at[side], recv_op.at[mine, :], number, sends0, recvs0)
        for number, (other, side) in enumerate(peers)
        if number >= 4
    ]
    recv_op[mine, :] = send_op[core]
    half_rows = parts * tile // 2
    near = rows_of(chip // 2, half_rows)
    away = rows_of(1 - chip // 2, half_rows)
    inner = jnp.logical_or(chip == 1, chip == 2)

    def relay(rows, number, slot):
        other, side = peers[number]
        return pltpu.make_async_remote_copy(
            src_ref=recv_op.at[rows, :],
            dst_ref=recv_op.at[rows, :],
            send_sem=sends0.at[slot],
            recv_sem=recvs0.at[slot],
            device_id=(freq, other * 2 + side),
            device_id_type=MESH,
        )

    first = []
    for chunk in range(chunks):
        loads[chunk].wait()

        def pack_field(to, carry):
            for focus in range(2):
                for source in range(4):
                    value = jnp.where(live[None], field[chunk, :, source, to, focus], 0.0)
                    block = coded(value, FIELD_SCALE).reshape(tile, 256)
                    lo = (focus * 4 + source) * 128
                    send1[chunk, 2 * to, :, lo:lo + 128] = block[:, :128]
                    send1[chunk, 2 * to + 1, :, lo:lo + 128] = block[:, 128:]
            return carry

        lax.fori_loop(0, chips, pack_field, 0)
        first.append([
            send(send1.at[chunk, other * 2 + side], recv1.at[chunk, mine, :], number,
                 sends1.at[chunk], recvs1.at[chunk])
            for number, (other, side) in enumerate(peers)
        ])
        recv1[chunk, mine, :] = send1[chunk, me]
        if chunk == 0:
            for copy in zeroth:
                copy.wait()

            @pl.when(inner)
            def _():
                relay(near, 2, 0).start()

    @pl.when(inner)
    def _():
        relay(near, 2, 0).wait()
        relay(away, 4, 1).start()

    column = lax.broadcasted_iota(jnp.int32, (length, 2 * length), 1)
    line = column // tile * rows_j + lax.rem(column, rows_j)
    pick = line == lax.broadcasted_iota(jnp.int32, (length, 2 * length), 0)
    owners = contract(
        jnp.broadcast_to(owner[...].astype(jnp.float32).astype(jnp.bfloat16), (8, length)),
        pick.astype(jnp.float32).astype(jnp.bfloat16),
        ((1,), (0,)),
    )[:1].astype(jnp.int32)
    across = lax.broadcasted_iota(jnp.int32, (2 * length, 2 * length), 1)
    down = lax.broadcasted_iota(jnp.int32, (2 * length, 2 * length), 0)
    wavenum = down // tile * rows_j + lax.rem(down, rows_j)
    quarter = lax.rem(down, tile) // rows_j - lax.rem(across, tile) // rows_j
    turns = lax.rem(wavenum * owners + (quarter + 4) * (length // 4), length)
    wheel = jnp.cos(turns.astype(jnp.float32) * (2.0 * math.pi / length))
    tables[0] = wheel * (1.0 / FIELD_SCALE)
    tables[1] = wheel.T * (1.0 / length)

    panel_load.wait()
    all_sources = raw.shape[0]

    def unpack_panel(block, carry):
        at = pl.ds(pl.multiple_of(block * 16, 16), 16)
        values = raw[at].astype(jnp.float32)
        for comp in range(2):
            half = values[:, comp, :].astype(jnp.bfloat16)
            for line in range(rows_j):
                for side in range(2):
                    lo = (line * 2 + side) * 128
                    panel[comp, side, at, line * 128:line * 128 + 128] = half[:, lo:lo + 128]
        return carry

    lax.fori_loop(0, all_sources // 16, unpack_panel, 0)

    @pl.when(inner)
    def _():
        relay(away, 4, 1).wait_send()

    @pl.when(jnp.logical_not(inner))
    def _():
        relay(away, 4, 1).wait_recv()

    for block in range(16):
        lo = block * 128
        weights[:, lo:lo + 128] = recv_op[:, lo:lo + 128].astype(jnp.float32) * (
            1.0 / OPERATOR_SCALE
        )

    second = []
    land_rows = rows_of(chip, 16)
    for chunk in range(chunks):
        for copy in first[chunk]:
            copy.wait()

        def transform(focus, carry):
            at = pl.ds(pl.multiple_of(focus * 512, 512), 512)
            values = recv1[chunk, :, at].astype(jnp.float32)
            spectrum = fine_dot(tables[0], values).reshape(parts, 2, rows_j, 512)
            real, imag = spectrum[:, 0], spectrum[:, 1]
            columns = []
            for target in range(4):
                out_real, out_imag = None, None
                for source in range(4):
                    lo = (target * 4 + source) * 128
                    weight = weights[:, lo:lo + 128].reshape(parts, 2, rows_j, 128)
                    wr, wi = weight[:, 0], weight[:, 1]
                    fr = real[:, :, source * 128:source * 128 + 128]
                    fi = imag[:, :, source * 128:source * 128 + 128]
                    tr = wr * fr - wi * fi
                    ti = wr * fi + wi * fr
                    out_real = tr if out_real is None else out_real + tr
                    out_imag = ti if out_imag is None else out_imag + ti
                columns.append(jnp.stack([out_real, out_imag], 1).reshape(2 * length, 128))
            wave = fine_dot(tables[1], jnp.concatenate(columns, 1))
            for part in range(parts):
                for comp in range(2):
                    for target in range(4):
                        lo = part * tile + comp * rows_j
                        start = part * rows_j * 16 + comp * 8 + target * 2 + focus
                        spread[pl.ds(start, rows_j, stride=16), :] = wave[
                            lo:lo + rows_j, target * 128:target * 128 + 128
                        ]
            return carry

        lax.fori_loop(0, 2, transform, 0)

        def pack_wave(part, carry):
            for line in range(rows_j):
                start = pl.multiple_of((part * rows_j + line) * 16, 16)
                send2[chunk, part, :, line * 128:line * 128 + 128] = spread[
                    pl.ds(start, 16), :
                ].astype(jnp.bfloat16)
            return carry

        lax.fori_loop(0, parts, pack_wave, 0)
        second.append([
            send(send2.at[chunk, other * 2 + side], recv2.at[chunk, core, land_rows, :], number,
                 sends2.at[chunk], recvs2.at[chunk])
            for number, (other, side) in enumerate(peers)
        ])
        recv2[chunk, core, land_rows, :] = send2[chunk, me]

    nt = ((1,), (1,))
    pieces = []
    for chunk in range(chunks):
        for copy in second[chunk]:
            copy.wait()
        wave0, wave1 = recv2[chunk, 0], recv2[chunk, 1]
        with_real = contract(wave0, panel[0, 0], nt) + contract(wave1, panel[0, 1], nt)
        with_imag = contract(wave0, panel[1, 0], nt) + contract(wave1, panel[1, 1], nt)
        for part in range(chips):
            lo = part * 16
            pieces.append(with_real[lo:lo + 8] - with_imag[lo + 8:lo + 16])
            pieces.append(with_real[lo + 8:lo + 16] + with_imag[lo:lo + 8])
    width = order.shape[0]
    if width > 8 * foci:
        pieces.append(jnp.zeros((width - 8 * foci, all_sources), jnp.float32))
    sources = joined.shape[1]
    total[...] = jnp.concatenate(pieces, 0).T.reshape(chips, 2, sources, width)
    third = send(total.at[:, 1 - core], twin, parts - 2, sends3, recvs3)
    third.wait()
    for to in range(chips):
        joined[to] = total[to, core] + twin[to]
    third = [
        send(joined.at[peers[number][0]], recv3.at[number // 2], number, sends3, recvs3)
        for number in (0, 2, 4)
    ]
    reflected = joined[chip]
    for copy in third:
        copy.wait()
    for number in range(chips - 1):
        reflected = reflected + recv3[number]

    weight = (freq + 1).astype(jnp.float32) * (2.0 / (freqs * (freqs + 1)))
    squares = lax.dot_general(
        jnp.ones((8, width), jnp.float32),
        reflected * reflected * weight,
        (nt, ((), ())),
        precision=HIGHEST,
        preferred_element_type=jnp.float32,
    )
    if sources < 128:
        squares = jnp.concatenate([squares, jnp.zeros((8, 128 - sources), jnp.float32)], 1)
    shared[0] = squares
    fourth = []
    for step in range(1, freqs):
        copy = pltpu.make_async_remote_copy(
            src_ref=shared.at[0],
            dst_ref=shared.at[step],
            send_sem=sends4.at[step],
            recv_sem=recvs4.at[step],
            device_id=(lax.rem(freq + step, freqs), me),
            device_id_type=MESH,
        )
        copy.start()
        fourth.append(copy)
    placed = lax.dot_general(
        reflected, order[...], (((1,), (0,)), ((), ())),
        precision=HIGHEST, preferred_element_type=jnp.float32,
    )
    channels = 4 * foci
    for comp in range(2):
        lo = comp * (placed.shape[1] // 2)
        focusing[:, comp, :] = direct[:, comp, :] - placed[:, lo:lo + channels]
    for copy in fourth:
        copy.wait()
    summed = shared[0]
    for step in range(1, freqs):
        summed = summed + shared[step]
    energy[...] = jnp.sqrt(summed[:1, :sources] / (2 * channels) + 1e-06)


def column_order(chips, group, width):
    foci = chips * group
    result = np.zeros((width, 2 * -(-4 * foci // 128) * 128), np.float32)
    here = 0
    for chunk in range(group // 2):
        for chip in range(chips):
            for comp in range(2):
                for target in range(4):
                    for focus in range(2):
                        at = target * foci + chip * group + chunk * 2 + focus
                        result[here, comp * (result.shape[1] // 2) + at] = 1.0
                        here += 1
    return result


def fused(field, live_count, line_owner, decomposer, reflection, direct_wave):
    freqs = lax.axis_size("freq")
    parts = lax.axis_size("line")
    foci = field.shape[3]
    rows_j = field.shape[4]
    length = line_owner.shape[0]
    chips = parts // 2
    group = foci // chips
    chunks = group // 2
    sources = direct_wave.shape[0]
    all_sources = reflection.shape[1]
    tile = 2 * rows_j
    width = -(-8 * foci // 128) * 128
    order = jnp.asarray(column_order(chips, group, width))

    vmem = pl.BlockSpec(memory_space=pltpu.VMEM)
    smem = pl.BlockSpec(memory_space=pltpu.SMEM)
    far = pl.BlockSpec(memory_space=pl.ANY)
    pair = pltpu.SemaphoreType.DMA((parts - 1,))
    many = pltpu.SemaphoreType.DMA((chunks, parts - 1))
    focusing, energy = pl.pallas_call(
        lambda *refs: update_kernel(freqs, parts, foci, rows_j, *refs),
        out_shape=(
            jax.ShapeDtypeStruct(direct_wave.shape[:1] + direct_wave.shape[2:], jnp.float32),
            jax.ShapeDtypeStruct((1, sources), jnp.float32),
        ),
        in_specs=[smem, vmem, far, vmem, far, vmem, vmem],
        out_specs=(vmem, vmem),
        scratch_shapes=[
            pltpu.VMEM((chunks, 2, 4, chips, 2, rows_j, 256), jnp.float32),
            pltpu.VMEM((2, tile, 2048), jnp.int16),
            pltpu.VMEM((parts * tile, 2048), jnp.int16),
            pltpu.VMEM((parts * tile, 2048), jnp.float32),
            pltpu.VMEM((chunks, parts, tile, 1024), jnp.int16),
            pltpu.VMEM((chunks, parts * tile, 1024), jnp.int16),
            pltpu.VMEM((2, 2 * length, 2 * length), jnp.float32),
            pltpu.VMEM(reflection.shape[1:], jnp.bfloat16),
            pltpu.VMEM((2, 2, all_sources, rows_j * 128), jnp.bfloat16),
            pltpu.VMEM((parts * rows_j * 16, 128), jnp.float32),
            pltpu.VMEM((chunks, parts, 16, rows_j * 128), jnp.bfloat16),
            pltpu.VMEM((chunks, 2, chips * 16, rows_j * 128), jnp.bfloat16),
            pltpu.VMEM((chips, 2, sources, width), jnp.float32),
            pltpu.VMEM((chips, sources, width), jnp.float32),
            pltpu.VMEM((chips, sources, width), jnp.float32),
            pltpu.VMEM((chips - 1, sources, width), jnp.float32),
            pltpu.VMEM((freqs, 8, 128), jnp.float32),
            pair, pair, many, many, many, many, pair, pair,
            pltpu.SemaphoreType.DMA((freqs,)),
            pltpu.SemaphoreType.DMA((freqs,)),
            pltpu.SemaphoreType.DMA((chunks + 1,)),
        ],
        compiler_params=pltpu.CompilerParams(
            collective_id=0, has_side_effects=True, vmem_limit_bytes=63 * 1024 * 1024
        ),
    )(
        live_count,
        line_owner[None],
        field.reshape(2, 4, chips, chunks, 2, rows_j, 256),
        decomposer[0],
        reflection[0],
        direct_wave[:, 0],
        order,
    )
    return focusing[:, None], energy[0]


def fits(field, line_owner, reflection, direct_wave):
    parts = lax.axis_size("line")
    rows_j = field.shape[4]
    foci = field.shape[3]
    return (
        parts == 8
        and rows_j == 8
        and field.shape[0] == 1
        and field.shape[5] == 256
        and foci % parts == 0
        and line_owner.shape[0] == parts * rows_j
        and direct_wave.shape[0] <= 128
        and direct_wave.shape[0] % 8 == 0
        and reflection.shape[1] % 256 == 0
        and reflection.shape[1] <= 512
    )


def phase_tables(line_owner, length):
    wavenum = jnp.arange(length, dtype=jnp.int32)
    products = wavenum[:, None] * line_owner[None, :] % length
    angles = products.astype(jnp.float32) * (2.0 * math.pi / length)
    return (jnp.cos(angles), jnp.sin(angles))


def decompose(operator, spectrum):
    real_rows = []
    imag_rows = []
    for target in range(4):
        real_sum = None
        imag_sum = None
        for source in range(4):
            weight_real = operator[:, 0, target, source][:, None]
            weight_imag = operator[:, 1, target, source][:, None]
            field_real = spectrum[:, 0, source]
            field_imag = spectrum[:, 1, source]
            term_real = weight_real * field_real - weight_imag * field_imag
            term_imag = weight_real * field_imag + weight_imag * field_real
            real_sum = term_real if real_sum is None else real_sum + term_real
            imag_sum = term_imag if imag_sum is None else imag_sum + term_imag
        real_rows.append(real_sum)
        imag_rows.append(imag_sum)
    return jnp.stack([jnp.stack(real_rows, 1), jnp.stack(imag_rows, 1)], 1)


def general(field, live_count, line_owner, decomposer, reflection, direct_wave):
    length = line_owner.shape[0]
    receivers = field.shape[5]
    cosine, sine_table = phase_tables(line_owner, length)
    forward_table = jnp.stack([jnp.stack([cosine, sine_table]), jnp.stack([-sine_table, cosine])])
    inverse_table = (
        jnp.stack([jnp.stack([cosine.T, -sine_table.T]), jnp.stack([sine_table.T, cosine.T])])
        / length
    )
    live_mask = jnp.arange(receivers, dtype=jnp.int32)[None, :] < live_count[:, None]
    live_field = jnp.where(live_mask, field, jnp.float32(0.0))
    operator = lax.all_gather(decomposer, "line", axis=4, tiled=True)
    every_line = lax.all_to_all(live_field, "line", split_axis=3, concat_axis=4, tiled=True)
    space_all = jnp.einsum(
        "yxjk,fxiokr->fyiojr",
        inverse_table,
        decompose(
            operator,
            jnp.einsum(
                "yxkj,fxiojr->fyiokr", forward_table, every_line, precision=lax.Precision.HIGHEST
            ),
        ),
        precision=lax.Precision.HIGHEST,
    )
    wavefield = lax.all_to_all(
        space_all.astype(jnp.bfloat16), "line", split_axis=4, concat_axis=3, tiled=True
    )
    freq_count = wavefield.shape[0]
    channels = wavefield.shape[2] * wavefield.shape[3]
    positions = wavefield.shape[4] * wavefield.shape[5]
    wave_bf = wavefield.reshape(freq_count, 2, channels, positions)
    real_part = wave_bf[:, 0]
    imag_part = wave_bf[:, 1]
    stacked = jnp.stack(
        [jnp.stack([real_part, imag_part], 1), jnp.stack([-imag_part, real_part], 1)], 1
    )
    reflected = lax.psum_scatter(
        jnp.einsum("fsxq,fxocq->sfoc", reflection, stacked, preferred_element_type=jnp.float32),
        "line",
        scatter_dimension=0,
        tiled=True,
    )
    focusing = direct_wave - reflected
    total_freqs = freq_count * lax.axis_size("freq")
    freq_index = lax.axis_index("freq") * freq_count + jnp.arange(freq_count, dtype=jnp.int32)
    weights = 2.0 * (freq_index + 1).astype(jnp.float32) / (total_freqs * (total_freqs + 1))
    partial_value = jnp.sum(jnp.sum(reflected * reflected, axis=(2, 3)) * weights[None, :], axis=1)
    energy_sum = lax.psum(partial_value, "freq")
    trace_energy = jnp.sqrt(energy_sum / (2 * channels) + 1e-06)
    return (focusing, trace_energy)


def on_device(field, live_count, line_owner, decomposer, reflection, direct_wave):
    if fits(field, line_owner, reflection, direct_wave):
        body = fused
    else:
        body = general
    return body(field, live_count, line_owner, decomposer, reflection, direct_wave)


def solution(mesh):
    return jax.shard_map(
        on_device,
        mesh=mesh,
        in_specs=(
            P("freq", None, None, None, "line", None),
            P("line"),
            P(),
            P("freq", None, None, None, "line", None),
            P("freq", None, None, "line"),
            P("line", "freq", None, None),
        ),
        out_specs=(P("line", "freq", None, None), P("line")),
        check_vma=False,
    )
```
